32 devices in a mesh: section: 4 (over y, x), seq: 2 (over core), dp: 4 (over z).
Axes of the slice: x: 2, y: 2, z: 4, core: 2. Of those that a mesh axis runs over, the one named last changes fastest.
Arguments:
- bases: int32 [8, 3072, 128], P('dp', 'seq'), may hold values from 0 to 3
- targets: int32 [8, 3072, 4096], P('dp', 'seq', 'section'), may hold values from 0 to 2
- stem_weight: bfloat16 [512, 384], replicated, may hold values from -0.5 to 0.5
- conv_weight: bfloat16 [4, 3, 384, 192], P('section'), may hold values from -0.1875 to 0.1875
- proj_weight: bfloat16 [4, 192, 384], P('section'), may hold values from -0.4375 to 0.4375
- head_weight: bfloat16 [384, 4096], P(None, 'section'), may hold values from -0.078125 to 0.078125
Outputs:
- conv_grad: float32 [4, 3, 384, 192], P('section')
- proj_grad: float32 [4, 192, 384], P('section')
- head_grad: float32 [384, 4096], P(None, 'section')
The draws below stay inside these ranges and needn't reach their ends.
All inputs are finite; a program needn't handle non-finite values.
Results may differ from the reference program's by a relative error of at most 0.0014.
Values may be sent and summed in bfloat16 or wider, within the bound.
A program may use at most 128 MiB of HBM per device.

```python
import math
import jax
import jax.numpy as jnp
from jax import lax

CHANNELS = 384
INNER = 192
BIN_BASES = 128
LEN = 3072
DILATION_START = 192
LAYERS = 4
OUTPUT_TRACKS = 4096
BATCH = 8
N_SECTION = 4


def touch_ends(result, key, least, high):
    place = [jax.random.randint(jax.random.fold_in(key, axis), (), 0, length) for axis, length in enumerate(result.shape)]
    longest = result.shape.index(max(result.shape))
    neighbour = place[:longest] + [(place[longest] + 1) % result.shape[longest]] + place[longest + 1:]
    return result.at[tuple(place)].set(least).at[tuple(neighbour)].set(high)


def level_of(stream_key, extent, split, smallest, largest):
    gain, own = 1.0, jax.random.fold_in(stream_key, 6)
    for dim, blocks in split:
        heights = jnp.exp(jax.random.uniform(jax.random.fold_in(own, dim), (blocks,), jnp.float32, smallest / len(split), largest / len(split)))
        gain = gain * jnp.repeat(heights, extent[dim] // blocks).reshape([-1 if axis == dim else 1 for axis in range(len(extent))])
    return gain


def normal_values(rng, dims, spread, most, pieces=(), held_as=jnp.bfloat16):
    drawn = jax.random.normal(rng, dims, jnp.float32) * spread
    if len(pieces) > 0:
        drawn = level_of(rng, dims, pieces, -0.22, 0.18) * drawn
    return jnp.clip(drawn, min=-most, max=most).astype(held_as)


def setup_inputs(seed: int = 0) -> dict:
    key_list = jax.random.split(jax.random.key(seed), 7)
    bases = touch_ends(jax.random.randint(key_list[0], (BATCH, LEN, BIN_BASES), 0, 4), jax.random.fold_in(key_list[0], 1), 0, 3).astype(jnp.int32)
    targets = touch_ends(jax.random.randint(key_list[1], (BATCH, LEN, OUTPUT_TRACKS), 0, 3), jax.random.fold_in(key_list[1], 1), 0, 2).astype(jnp.int32)
    stem_weight = normal_values(key_list[2], (4 * BIN_BASES, CHANNELS), BIN_BASES ** -0.5, 0.5)
    conv_weight = normal_values(key_list[3], (LAYERS, 3, CHANNELS, INNER), (3 * CHANNELS) ** -0.5, 0.1875, ((0, 4),))
    proj_weight = normal_values(key_list[4], (LAYERS, INNER, CHANNELS), INNER ** -0.5, 0.4375, ((0, 4),))
    head_weight = normal_values(key_list[5], (CHANNELS, OUTPUT_TRACKS), (16 * CHANNELS) ** -0.5, 0.078125, ((1, 4),))
    return dict(bases=bases, targets=targets, stem_weight=stem_weight, conv_weight=conv_weight, proj_weight=proj_weight, head_weight=head_weight)


SQRT_TWO_OVER_PI = 0.7978845608028654
CUBIC_TERM = 0.044715

def gelu_value(inputs):
    return 0.5 * inputs * (1.0 + jnp.tanh(SQRT_TWO_OVER_PI * (inputs + CUBIC_TERM * inputs * inputs * inputs)))

def gelu_slope(inputs):
    tangent = jnp.tanh(SQRT_TWO_OVER_PI * (inputs + CUBIC_TERM * inputs * inputs * inputs))
    return 0.5 * (1.0 + tangent) + 0.5 * inputs * (1.0 - tangent * tangent) * SQRT_TWO_OVER_PI * (1.0 + 3.0 * CUBIC_TERM * inputs * inputs)

def flatten(values):
    return values.reshape(-1, values.shape[-1])

def contract_rows(left_side, right_side):
    return lax.dot_general(flatten(left_side), flatten(right_side), (((0,), (0,)), ((), ())), preferred_element_type=jnp.float32)

def times_transposed(left_side, right_side):
    return lax.dot_general(left_side, right_side, (((1,), (1,)), ((), ())), preferred_element_type=jnp.float32)

def shifted(values, dilation_rate):
    padding = jnp.zeros((values.shape[0], dilation_rate, values.shape[2]), values.dtype)
    behind = jnp.concatenate([padding, values[:, :-dilation_rate]], 1)
    forward = jnp.concatenate([values[:, dilation_rate:], padding], 1)
    return (behind, forward)

def reference(bases, targets, stem_weight, conv_weight, proj_weight, head_weight):
    batch_count, seq_len, bin_width = bases.shape
    channels = stem_weight.shape[1]
    inner_width = proj_weight.shape[1]
    letters = jnp.arange(4, dtype=jnp.int32)
    onehot = (bases[..., None] == letters).astype(jnp.bfloat16).reshape(batch_count * seq_len, bin_width * 4)
    state = jnp.dot(onehot, stem_weight, preferred_element_type=jnp.float32).astype(jnp.bfloat16)
    state = state.reshape(batch_count, seq_len, channels)
    saved_list = []
    for layer_position in range(N_SECTION):
        dilation_rate = DILATION_START * 2 ** layer_position
        kernel = conv_weight[layer_position]
        hidden = gelu_value(state.astype(jnp.float32)).astype(jnp.bfloat16)
        behind, forward = shifted(hidden, dilation_rate)
        inner_sum = jnp.dot(flatten(behind), kernel[0], preferred_element_type=jnp.float32)
        inner_sum = inner_sum + jnp.dot(flatten(hidden), kernel[1], preferred_element_type=jnp.float32)
        inner_sum = inner_sum + jnp.dot(flatten(forward), kernel[2], preferred_element_type=jnp.float32)
        active = gelu_value(inner_sum).astype(jnp.bfloat16)
        saved_list.append((state, hidden, behind, forward, inner_sum))
        update = jnp.dot(active, proj_weight[layer_position], preferred_element_type=jnp.float32)
        state = (flatten(state).astype(jnp.float32) + update).astype(jnp.bfloat16).reshape(batch_count, seq_len, channels)
    lifted = gelu_value(state.astype(jnp.float32)).astype(jnp.bfloat16)
    factor = 1.0 / math.sqrt(batch_count * seq_len)

    def head_step(running, item_pair):
        lifted_one, target_one = item_pair
        logits = jnp.dot(lifted_one, head_weight, preferred_element_type=jnp.float32)
        slope = ((jnp.exp(logits) - target_one.astype(jnp.float32)) * factor).astype(jnp.bfloat16)
        return (running + contract_rows(lifted_one, slope), times_transposed(slope, head_weight))
    head_grad, lift_grad = lax.scan(head_step, jnp.zeros((channels, head_weight.shape[1]), jnp.float32), (lifted, targets))
    cotangent = (lift_grad * gelu_slope(state.astype(jnp.float32))).astype(jnp.bfloat16)
    conv_list = []
    proj_list = []
    for layer_position in reversed(range(N_SECTION)):
        dilation_rate = DILATION_START * 2 ** layer_position
        kernel = conv_weight[layer_position]
        start_state, hidden, behind, forward, inner_sum = saved_list[layer_position]
        active = gelu_value(inner_sum).astype(jnp.bfloat16)
        proj_list.append(contract_rows(active, cotangent))
        active_grad = times_transposed(flatten(cotangent), proj_weight[layer_position])
        inner_grad = (active_grad * gelu_slope(inner_sum)).astype(jnp.bfloat16)
        inner_grad = inner_grad.reshape(batch_count, seq_len, inner_width)
        conv_list.append(jnp.stack([contract_rows(behind, inner_grad), contract_rows(hidden, inner_grad), contract_rows(forward, inner_grad)]))
        grad_behind, grad_forward = shifted(inner_grad, dilation_rate)
        hidden_grad = times_transposed(flatten(inner_grad), kernel[1])
        hidden_grad = hidden_grad + times_transposed(flatten(grad_forward), kernel[0])
        hidden_grad = hidden_grad + times_transposed(flatten(grad_behind), kernel[2])
        merged = flatten(cotangent).astype(jnp.float32) + hidden_grad * gelu_slope(flatten(start_state).astype(jnp.float32))
        cotangent = merged.astype(jnp.bfloat16).reshape(batch_count, seq_len, channels)
    conv_grad = jnp.stack(conv_list[::-1])
    proj_grad = jnp.stack(proj_list[::-1])
    return (conv_grad, proj_grad, head_grad)
```

```python
import math

import jax
import jax.numpy as jnp
from jax import lax
from jax.sharding import PartitionSpec as P

SQRT_TWO_OVER_PI = 0.7978845608028654
CUBIC_TERM = 0.044715


def gelu_value(inputs):
    return (
        0.5
        * inputs
        * (1.0 + jnp.tanh(SQRT_TWO_OVER_PI * (inputs + CUBIC_TERM * inputs * inputs * inputs)))
    )


def gelu_slope(inputs):
    tangent = jnp.tanh(SQRT_TWO_OVER_PI * (inputs + CUBIC_TERM * inputs * inputs * inputs))
    return 0.5 * (1.0 + tangent) + 0.5 * inputs * (1.0 - tangent * tangent) * SQRT_TWO_OVER_PI * (
        1.0 + 3.0 * CUBIC_TERM * inputs * inputs
    )


def contract_rows(left_side, right_side):
    return lax.dot_general(
        left_side, right_side, (((0,), (0,)), ((), ())), preferred_element_type=jnp.float32
    )


def times_transposed(left_side, right_side):
    return lax.dot_general(
        left_side, right_side, (((1,), (1,)), ((), ())), preferred_element_type=jnp.float32
    )


def shift_rows(value, by):
    if abs(by) >= value.shape[0]:
        return jnp.zeros_like(value)
    pad = jnp.zeros((abs(by),) + value.shape[1:], value.dtype)
    if by > 0:
        return jnp.concatenate([pad, value[:-by]], 0)
    return jnp.concatenate([value[-by:], pad], 0)


def body(bases, targets, stem_weight, conv_weight, proj_weight, head_weight):
    sections = lax.axis_size("section")
    seqs = lax.axis_size("seq")
    section_number = lax.axis_index("section")
    batches, row_count, bin_width = bases.shape
    channels = stem_weight.shape[1]
    length = row_count * seqs
    factor = 1.0 / math.sqrt(batches * lax.axis_size("dp") * length)
    unit = length // 2**sections
    local_q = row_count // unit
    blocks = length // unit
    columns = batches * unit // (seqs * sections)

    conv_all = lax.all_gather(conv_weight, "section", axis=0, tiled=True)
    proj_all = lax.all_gather(proj_weight, "section", axis=0, tiled=True)

    def to_chains(value):
        value = lax.all_to_all(value, "seq", split_axis=1, concat_axis=0, tiled=True)
        return value.reshape(blocks * columns, value.shape[-1])

    own = bases.reshape(batches, local_q, unit, bin_width).transpose(1, 0, 2, 3)
    own = own.reshape(local_q, seqs, sections, columns, bin_width)
    own = lax.dynamic_index_in_dim(own, section_number, 2, keepdims=False)
    picked = to_chains(own.astype(jnp.bfloat16))
    onehot = jnp.concatenate([(picked == c).astype(jnp.bfloat16) for c in range(4)], 1)
    stem = stem_weight.reshape(bin_width, 4, channels).transpose(1, 0, 2).reshape(-1, channels)
    state = jnp.dot(onehot, stem, preferred_element_type=jnp.float32).astype(jnp.bfloat16)

    saved = []
    for layer in range(sections):
        by = columns * 2**layer
        taps = conv_all[layer].reshape(-1, conv_all.shape[-1])
        hidden = gelu_value(state.astype(jnp.float32)).astype(jnp.bfloat16)
        wide = jnp.concatenate([shift_rows(hidden, by), hidden, shift_rows(hidden, -by)], 1)
        inner_sum = jnp.dot(wide, taps, preferred_element_type=jnp.float32)
        active = gelu_value(inner_sum).astype(jnp.bfloat16)
        update = jnp.dot(active, proj_all[layer], preferred_element_type=jnp.float32)
        saved.append((state, wide, inner_sum, active))
        state = (state.astype(jnp.float32) + update).astype(jnp.bfloat16)

    lifted = gelu_value(state.astype(jnp.float32)).astype(jnp.bfloat16)
    lifted = lifted.reshape(seqs, local_q, 1, columns, channels)
    lifted = lax.all_to_all(lifted, "seq", split_axis=0, concat_axis=2, tiled=True)
    lifted = lifted.reshape(local_q, seqs, 1, columns, channels)
    lifted = lax.all_gather(lifted, "section", axis=2, tiled=True)
    lifted = lifted.reshape(local_q, batches, unit, channels).transpose(1, 0, 2, 3)
    lifted = lifted.reshape(batches * row_count, channels)

    logits = jnp.dot(lifted, head_weight, preferred_element_type=jnp.float32)
    counts = targets.reshape(batches * row_count, targets.shape[2]).astype(jnp.float32)
    slope = ((jnp.exp(logits) - counts) * factor).astype(jnp.bfloat16)
    head_grad = contract_rows(lifted, slope)
    lift_part = times_transposed(slope, head_weight)

    lift_part = lift_part.reshape(batches, local_q, unit, channels).transpose(1, 0, 2, 3)
    lift_part = lift_part.reshape(local_q, seqs, sections, columns, channels)
    lift_part = lax.psum_scatter(lift_part, "section", scatter_dimension=2, tiled=True)
    lift_grad = to_chains(lift_part.reshape(local_q, seqs, columns, channels))

    grad = (lift_grad * gelu_slope(state.astype(jnp.float32))).astype(jnp.bfloat16)
    conv_list, proj_list = [], []
    for layer in reversed(range(sections)):
        by = columns * 2**layer
        start_state, wide, inner_sum, active = saved[layer]
        kernel = conv_all[layer]
        proj_list.append(contract_rows(active, grad))
        active_grad = times_transposed(grad, proj_all[layer])
        inner_grad = (active_grad * gelu_slope(inner_sum)).astype(jnp.bfloat16)
        conv_list.append(contract_rows(wide, inner_grad).reshape(kernel.shape))
        wide_grad = jnp.concatenate(
            [shift_rows(inner_grad, -by), inner_grad, shift_rows(inner_grad, by)], 1
        )
        turned = kernel.transpose(0, 2, 1).reshape(-1, channels)
        hidden_grad = jnp.dot(wide_grad, turned, preferred_element_type=jnp.float32)
        grad = (
            grad.astype(jnp.float32) + hidden_grad * gelu_slope(start_state.astype(jnp.float32))
        ).astype(jnp.bfloat16)
    conv_part = lax.psum_scatter(
        jnp.stack(conv_list[::-1]), "section", scatter_dimension=0, tiled=True
    )
    proj_part = lax.psum_scatter(
        jnp.stack(proj_list[::-1]), "section", scatter_dimension=0, tiled=True
    )
    return lax.psum((conv_part, proj_part, head_grad), ("seq", "dp"))


def solution(mesh):
    in_specs = (
        P("dp", "seq", None),
        P("dp", "seq", "section"),
        P(),
        P("section", None, None, None),
        P("section", None, None),
        P(None, "section"),
    )
    out_specs = (P("section", None, None, None), P("section", None, None), P(None, "section"))
    return jax.shard_map(body, mesh=mesh, in_specs=in_specs, out_specs=out_specs, check_vma=False)
```

```python
import math

import jax
import jax.numpy as jnp
from jax import lax
from jax.experimental import pallas as pl
from jax.experimental.pallas import tpu as pltpu
from jax.sharding import PartitionSpec as P

SQRT_TWO_OVER_PI = 0.7978845608028654
CUBIC_TERM = 0.044715


def gelu_value(inputs):
    return (
        0.5
        * inputs
        * (1.0 + jnp.tanh(SQRT_TWO_OVER_PI * (inputs + CUBIC_TERM * inputs * inputs * inputs)))
    )


def gelu_slope(inputs):
    tangent = jnp.tanh(SQRT_TWO_OVER_PI * (inputs + CUBIC_TERM * inputs * inputs * inputs))
    return 0.5 * (1.0 + tangent) + 0.5 * inputs * (1.0 - tangent * tangent) * SQRT_TWO_OVER_PI * (
        1.0 + 3.0 * CUBIC_TERM * inputs * inputs
    )


def contract_rows(left_side, right_side):
    return lax.dot_general(
        left_side, right_side, (((0,), (0,)), ((), ())), preferred_element_type=jnp.float32
    )


def times_transposed(left_side, right_side):
    return lax.dot_general(
        left_side, right_side, (((1,), (1,)), ((), ())), preferred_element_type=jnp.float32
    )


def shift_rows(value, by):
    if abs(by) >= value.shape[0]:
        return jnp.zeros_like(value)
    pad = jnp.zeros((abs(by),) + value.shape[1:], value.dtype)
    if by > 0:
        return jnp.concatenate([pad, value[:-by]], 0)
    return jnp.concatenate([value[-by:], pad], 0)


MESH = pl.DeviceIdType.MESH
ANY = pl.BlockSpec(memory_space=pl.ANY)


def greet(peers):
    barrier = pltpu.get_barrier_semaphore()
    for peer in peers:
        pl.semaphore_signal(barrier, inc=1, device_id=peer, device_id_type=MESH)
    pl.semaphore_wait(barrier, len(peers))


def remote(src, dst, send, recv, peer):
    return pltpu.make_async_remote_copy(
        src_ref=src, dst_ref=dst, send_sem=send, recv_sem=recv, device_id=peer, device_id_type=MESH
    )


def gather_weights(conv, proj, sections):
    def kernel(conv_ref, proj_ref, conv_out, proj_out, send, recv, local, send2, recv2):
        s, c = lax.axis_index("section"), lax.axis_index("seq")
        others = [lax.rem(s + k, sections) for k in range(1, sections)]
        partner = {"section": s, "seq": 1 - c}
        peers = [{"section": o, "seq": c} for o in others]
        greet(peers + [partner])
        pairs = ((conv_ref, conv_out), (proj_ref, proj_out))
        first, second, own = [], [], []
        for k, peer in enumerate(peers):
            for n, (src, out) in enumerate(pairs):
                first.append(remote(src.at[c], out.at[s, c], send.at[k, n], recv.at[k, n], peer))
                first[-1].start()
        for n, (src, out) in enumerate(pairs):
            own.append(pltpu.make_async_copy(src, out.at[s], local.at[n]))
            own[-1].start()
        for k in range(sections - 1):
            source = lax.rem(s + sections - 1 - k, sections)
            for n, (_, out) in enumerate(pairs):
                first[2 * k + n].wait_recv()
                piece = out.at[source, c]
                second.append(remote(piece, piece, send2.at[k, n], recv2.at[k, n], partner))
                second[-1].start()
        for copy in second:
            copy.wait()
        for copy in first:
            copy.wait_send()
        for copy in own:
            copy.wait()

    sems = pltpu.SemaphoreType.DMA((sections - 1, 2))
    return pl.pallas_call(
        kernel,
        out_shape=[
            jax.ShapeDtypeStruct((sections,) + conv.shape, conv.dtype),
            jax.ShapeDtypeStruct((sections,) + proj.shape, proj.dtype),
        ],
        in_specs=[ANY] * 2,
        out_specs=[ANY] * 2,
        scratch_shapes=[sems, sems, pltpu.SemaphoreType.DMA((2,)), sems, sems],
        compiler_params=pltpu.CompilerParams(collective_id=0, has_side_effects=True),
    )(conv, proj)


def exchange(value, sections, seqs, columns, to_head):
    group = sections * seqs

    def kernel(src, out, send, recv, local):
        s, c = lax.axis_index("section"), lax.axis_index("seq")
        me = s * seqs + c

        def part(ref, batch, section):
            start = pl.multiple_of(section * columns, 16)
            return ref.at[batch, :, pl.ds(start, columns), :]

        def ends(ps, pc):
            if to_head:
                return src.at[pc], part(out, c, s)
            return part(src, pc, ps), out.at[s, c]

        places = []
        for k in range(1, group):
            p = lax.rem(me + k, group)
            places.append((p // seqs, lax.rem(p, seqs)))
        peers = [{"section": ps, "seq": pc} for ps, pc in places]
        greet(peers)
        copies = []
        for k, (ps, pc) in enumerate(places):
            source, target = ends(ps, pc)
            copies.append(remote(source, target, send.at[k], recv.at[k], peers[k]))
            copies[-1].start()
        source, target = ends(s, c)
        own = pltpu.make_async_copy(source, target, local)
        own.start()
        own.wait()
        for copy in copies:
            copy.wait()

    q, channels = value.shape[1], value.shape[3]
    if to_head:
        shape = (seqs, q, sections * columns, channels)
    else:
        shape = (sections, seqs, q, columns, channels)
    sems = pltpu.SemaphoreType.DMA((group - 1,))
    return pl.pallas_call(
        kernel,
        out_shape=jax.ShapeDtypeStruct(shape, value.dtype),
        in_specs=[ANY],
        out_specs=ANY,
        scratch_shapes=[sems, sems, pltpu.SemaphoreType.DMA],
        compiler_params=pltpu.CompilerParams(
            collective_id=1 if to_head else 2, has_side_effects=True
        ),
    )(value)


def body(bases, targets, stem_weight, conv_weight, proj_weight, head_weight):
    sections = lax.axis_size("section")
    seqs = lax.axis_size("seq")
    section_number = lax.axis_index("section")
    batches, row_count, bin_width = bases.shape
    channels = stem_weight.shape[1]
    length = row_count * seqs
    factor = 1.0 / math.sqrt(batches * lax.axis_size("dp") * length)
    unit = length // 2**sections
    local_q = row_count // unit
    blocks = length // unit
    columns = batches * unit // (seqs * sections)

    paired = seqs == 2 and batches == seqs and columns % 16 == 0

    if paired:
        conv_all, proj_all = gather_weights(
            conv_weight.reshape(2, -1, conv_weight.shape[-1]),
            proj_weight.reshape(2, -1, channels),
            sections,
        )
        conv_all = conv_all.reshape((sections,) + conv_weight.shape[1:])
        proj_all = proj_all.reshape((sections,) + proj_weight.shape[1:])
    else:
        conv_all = lax.all_gather(conv_weight, "section", axis=0, tiled=True)
        proj_all = lax.all_gather(proj_weight, "section", axis=0, tiled=True)

    def to_chains(value):
        value = lax.all_to_all(value, "seq", split_axis=1, concat_axis=0, tiled=True)
        return value.reshape(blocks * columns, value.shape[-1])

    own = bases.reshape(batches, local_q, unit, bin_width).transpose(1, 0, 2, 3)
    own = own.reshape(local_q, seqs, sections, columns, bin_width)
    own = lax.dynamic_index_in_dim(own, section_number, 2, keepdims=False)
    picked = to_chains(own.astype(jnp.bfloat16))
    onehot = jnp.concatenate([(picked == c).astype(jnp.bfloat16) for c in range(4)], 1)
    stem = stem_weight.reshape(bin_width, 4, channels).transpose(1, 0, 2).reshape(-1, channels)
    state = jnp.dot(onehot, stem, preferred_element_type=jnp.float32).astype(jnp.bfloat16)

    saved = []
    for layer in range(sections):
        by = columns * 2**layer
        taps = conv_all[layer].reshape(-1, conv_all.shape[-1])
        hidden = gelu_value(state.astype(jnp.float32)).astype(jnp.bfloat16)
        wide = jnp.concatenate([shift_rows(hidden, by), hidden, shift_rows(hidden, -by)], 1)
        inner_sum = jnp.dot(wide, taps, preferred_element_type=jnp.float32)
        active = gelu_value(inner_sum).astype(jnp.bfloat16)
        update = jnp.dot(active, proj_all[layer], preferred_element_type=jnp.float32)
        saved.append((state, wide, inner_sum, active))
        state = (state.astype(jnp.float32) + update).astype(jnp.bfloat16)

    lifted = gelu_value(state.astype(jnp.float32)).astype(jnp.bfloat16)
    if paired:
        lifted = lifted.reshape(seqs, local_q, columns, channels)
        lifted = exchange(lifted, sections, seqs, columns, True)
    else:
        lifted = lifted.reshape(seqs, local_q, 1, columns, channels)
        lifted = lax.all_to_all(lifted, "seq", split_axis=0, concat_axis=2, tiled=True)
        lifted = lifted.reshape(local_q, seqs, 1, columns, channels)
        lifted = lax.all_gather(lifted, "section", axis=2, tiled=True)
        lifted = lifted.reshape(local_q, batches, unit, channels).transpose(1, 0, 2, 3)
    lifted = lifted.reshape(batches * row_count, channels)

    logits = jnp.dot(lifted, head_weight, preferred_element_type=jnp.float32)
    counts = targets.reshape(batches * row_count, targets.shape[2]).astype(jnp.float32)
    slope = ((jnp.exp(logits) - counts) * factor).astype(jnp.bfloat16)
    head_sum = lax.psum(contract_rows(lifted, slope), ("seq", "dp"))
    lift_part = times_transposed(slope, head_weight)

    if paired:
        lift_part = lift_part.astype(jnp.bfloat16).reshape(batches, local_q, unit, channels)
        terms = exchange(lift_part, sections, seqs, columns, False)
        lift_grad = terms.astype(jnp.float32).sum(0).reshape(blocks * columns, channels)
    else:
        lift_part = lift_part.reshape(batches, local_q, unit, channels).transpose(1, 0, 2, 3)
        lift_part = lift_part.reshape(local_q, seqs, sections, columns, channels)
        lift_part = lax.psum_scatter(lift_part, "section", scatter_dimension=2, tiled=True)
        lift_grad = to_chains(lift_part.reshape(local_q, seqs, columns, channels))

    grad = (lift_grad * gelu_slope(state.astype(jnp.float32))).astype(jnp.bfloat16)
    conv_list, proj_list = [], []
    for layer in reversed(range(sections)):
        by = columns * 2**layer
        start_state, wide, inner_sum, active = saved[layer]
        kernel = conv_all[layer]
        proj_list.append(contract_rows(active, grad))
        active_grad = times_transposed(grad, proj_all[layer])
        inner_grad = (active_grad * gelu_slope(inner_sum)).astype(jnp.bfloat16)
        conv_list.append(contract_rows(wide, inner_grad).reshape(kernel.shape))
        wide_grad = jnp.concatenate(
            [shift_rows(inner_grad, -by), inner_grad, shift_rows(inner_grad, by)], 1
        )
        turned = kernel.transpose(0, 2, 1).reshape(-1, channels)
        hidden_grad = jnp.dot(wide_grad, turned, preferred_element_type=jnp.float32)
        grad = (
            grad.astype(jnp.float32) + hidden_grad * gelu_slope(start_state.astype(jnp.float32))
        ).astype(jnp.bfloat16)
    conv_part = lax.psum_scatter(
        jnp.stack(conv_list[::-1]), "section", scatter_dimension=0, tiled=True
    )
    proj_part = lax.psum_scatter(
        jnp.stack(proj_list[::-1]), "section", scatter_dimension=0, tiled=True
    )
    conv_part, proj_part, head_sum = lax.optimization_barrier((conv_part, proj_part, head_sum))
    return lax.psum((conv_part, proj_part), ("seq", "dp")) + (head_sum,)


def solution(mesh):
    in_specs = (
        P("dp", "seq", None),
        P("dp", "seq", "section"),
        P(),
        P("section", None, None, None),
        P("section", None, None),
        P(None, "section"),
    )
    out_specs = (P("section", None, None, None), P("section", None, None), P(None, "section"))
    return jax.shard_map(body, mesh=mesh, in_specs=in_specs, out_specs=out_specs, check_vma=False)
```

```python
import math

import jax
import jax.numpy as jnp
from jax import lax
from jax.experimental import pallas as pl
from jax.experimental.pallas import tpu as pltpu
from jax.sharding import PartitionSpec as P

SQRT_TWO_OVER_PI = 0.7978845608028654
CUBIC_TERM = 0.044715


def gelu_value(inputs):
    return (
        0.5
        * inputs
        * (1.0 + jnp.tanh(SQRT_TWO_OVER_PI * (inputs + CUBIC_TERM * inputs * inputs * inputs)))
    )


def gelu_slope(inputs):
    tangent = jnp.tanh(SQRT_TWO_OVER_PI * (inputs + CUBIC_TERM * inputs * inputs * inputs))
    return 0.5 * (1.0 + tangent) + 0.5 * inputs * (1.0 - tangent * tangent) * SQRT_TWO_OVER_PI * (
        1.0 + 3.0 * CUBIC_TERM * inputs * inputs
    )


def contract_rows(left_side, right_side):
    return lax.dot_general(
        left_side, right_side, (((0,), (0,)), ((), ())), preferred_element_type=jnp.float32
    )


def times_transposed(left_side, right_side):
    return lax.dot_general(
        left_side, right_side, (((1,), (1,)), ((), ())), preferred_element_type=jnp.float32
    )


def shift_rows(value, by):
    if abs(by) >= value.shape[0]:
        return jnp.zeros_like(value)
    pad = jnp.zeros((abs(by),) + value.shape[1:], value.dtype)
    if by > 0:
        return jnp.concatenate([pad, value[:-by]], 0)
    return jnp.concatenate([value[-by:], pad], 0)


MESH = pl.DeviceIdType.MESH
ANY = pl.BlockSpec(memory_space=pl.ANY)


def greet(peers):
    barrier = pltpu.get_barrier_semaphore()
    for peer in peers:
        pl.semaphore_signal(barrier, inc=1, device_id=peer, device_id_type=MESH)
    pl.semaphore_wait(barrier, len(peers))


def remote(src, dst, send, recv, peer):
    return pltpu.make_async_remote_copy(
        src_ref=src, dst_ref=dst, send_sem=send, recv_sem=recv, device_id=peer, device_id_type=MESH
    )


def gather_weights(conv, proj, sections):
    def kernel(conv_ref, proj_ref, conv_out, proj_out, send, recv, local, send2, recv2):
        s, c = lax.axis_index("section"), lax.axis_index("seq")
        others = [lax.rem(s + k, sections) for k in range(1, sections)]
        partner = {"section": s, "seq": 1 - c}
        peers = [{"section": o, "seq": c} for o in others]
        greet(peers + [partner])
        pairs = ((conv_ref, conv_out), (proj_ref, proj_out))
        first, second, own = [], [], []
        for k, peer in enumerate(peers):
            for n, (src, out) in enumerate(pairs):
                first.append(remote(src.at[c], out.at[s, c], send.at[k, n], recv.at[k, n], peer))
                first[-1].start()
        for n, (src, out) in enumerate(pairs):
            own.append(pltpu.make_async_copy(src, out.at[s], local.at[n]))
            own[-1].start()
        for k in range(sections - 1):
            source = lax.rem(s + sections - 1 - k, sections)
            for n, (_, out) in enumerate(pairs):
                first[2 * k + n].wait_recv()
                piece = out.at[source, c]
                second.append(remote(piece, piece, send2.at[k, n], recv2.at[k, n], partner))
                second[-1].start()
        for copy in second:
            copy.wait()
        for copy in first:
            copy.wait_send()
        for copy in own:
            copy.wait()

    sems = pltpu.SemaphoreType.DMA((sections - 1, 2))
    return pl.pallas_call(
        kernel,
        out_shape=[
            jax.ShapeDtypeStruct((sections,) + conv.shape, conv.dtype),
            jax.ShapeDtypeStruct((sections,) + proj.shape, proj.dtype),
        ],
        in_specs=[ANY] * 2,
        out_specs=[ANY] * 2,
        scratch_shapes=[sems, sems, pltpu.SemaphoreType.DMA((2,)), sems, sems],
        compiler_params=pltpu.CompilerParams(collective_id=0, has_side_effects=True),
    )(conv, proj)


def exchange(value, sections, seqs, columns, to_head):
    group = sections * seqs

    def kernel(src, out, send, recv, local):
        s, c = lax.axis_index("section"), lax.axis_index("seq")
        me = s * seqs + c

        def part(ref, batch, section):
            start = pl.multiple_of(section * columns, 16)
            return ref.at[batch, :, pl.ds(start, columns), :]

        def ends(ps, pc):
            if to_head:
                return src.at[pc], part(out, c, s)
            return part(src, pc, ps), out.at[s, c]

        places = []
        for k in range(1, group):
            p = lax.rem(me + k, group)
            places.append((p // seqs, lax.rem(p, seqs)))
        peers = [{"section": ps, "seq": pc} for ps, pc in places]
        greet(peers)
        copies = []
        for k, (ps, pc) in enumerate(places):
            source, target = ends(ps, pc)
            copies.append(remote(source, target, send.at[k], recv.at[k], peers[k]))
            copies[-1].start()
        source, target = ends(s, c)
        own = pltpu.make_async_copy(source, target, local)
        own.start()
        own.wait()
        for copy in copies:
            copy.wait()

    q, channels = value.shape[1], value.shape[3]
    if to_head:
        shape = (seqs, q, sections * columns, channels)
    else:
        shape = (sections, seqs, q, columns, channels)
    sems = pltpu.SemaphoreType.DMA((group - 1,))
    return pl.pallas_call(
        kernel,
        out_shape=jax.ShapeDtypeStruct(shape, value.dtype),
        in_specs=[ANY],
        out_specs=ANY,
        scratch_shapes=[sems, sems, pltpu.SemaphoreType.DMA],
        compiler_params=pltpu.CompilerParams(
            collective_id=1 if to_head else 2, has_side_effects=True
        ),
    )(value)


def sum_gradients(value, sections, zones):
    rows, width = value.shape[1:]
    half = rows // 2
    piece = half // zones

    def kernel(
        src, out, met, wire, came, total, zcame, s0, r0, s1, r1, s2, r2, s3, r3, s4, r4
    ):
        s, c, d = (lax.axis_index(name) for name in ("section", "seq", "dp"))
        partner = {"section": s, "seq": 1 - c, "dp": d}
        order = [lax.rem(s + k, sections) for k in range(1, sections + 1)]
        across = [{"section": o, "seq": c, "dp": d} for o in order[:-1]]
        levels = [lax.rem(d + k, zones) for k in range(1, zones)]
        along = [{"section": s, "seq": c, "dp": z} for z in levels]
        greet([partner] + across + along)

        def strip(z):
            return pl.ds(pl.multiple_of(z * piece, 8), piece)

        def far(o):
            return src.at[o, pl.ds(pl.multiple_of((1 - c) * half, 8), half), :]

        def near(o):
            return src[o, pl.ds(pl.multiple_of(c * half, 8), half), :]

        pair = [remote(far(o), met.at[k], s0.at[k], r0.at[k], partner) for k, o in enumerate(order)]
        for copy in pair:
            copy.start()
        hops = []
        for k, peer in enumerate(across):
            pair[k].wait_recv()
            wire[k] = (met[k] + near(order[k])).astype(wire.dtype)
            hops.append(remote(wire.at[k], came.at[k], s1.at[k], r1.at[k], peer))
            hops[-1].start()
        pair[sections - 1].wait_recv()
        total[...] = met[sections - 1] + near(order[sections - 1])
        for k, copy in enumerate(hops):
            copy.wait_recv()
            total[...] += came[k].astype(jnp.float32)
        climbs = []
        for k, peer in enumerate(along):
            climbs.append(
                remote(total.at[strip(levels[k])], zcame.at[k], s2.at[k], r2.at[k], peer)
            )
            climbs[-1].start()
        done = total[strip(d), :]
        for k, copy in enumerate(climbs):
            copy.wait_recv()
            done = done + zcame[k]
        out[c, strip(d), :] = done

        mine = out.at[c, strip(d)]
        backs = [remote(mine, mine, s3.at[k], r3.at[k], peer) for k, peer in enumerate(along)]
        for copy in backs:
            copy.start()
        ends = [remote(mine, mine, s4.at[0], r4.at[0], partner)]
        ends[0].start()
        for k in range(zones - 1):
            backs[k].wait_recv()
            landed = out.at[c, strip(lax.rem(d + zones - 1 - k, zones))]
            ends.append(remote(landed, landed, s4.at[k + 1], r4.at[k + 1], partner))
            ends[-1].start()
        for copy in ends:
            copy.wait()
        for copy in pair + hops + climbs + backs:
            copy.wait_send()

    def dma(count):
        return [pltpu.SemaphoreType.DMA((count,))] * 2

    out = pl.pallas_call(
        kernel,
        out_shape=jax.ShapeDtypeStruct((2, half, width), jnp.float32),
        in_specs=[pl.BlockSpec(memory_space=pltpu.VMEM)],
        out_specs=pl.BlockSpec(memory_space=pltpu.VMEM),
        scratch_shapes=[
            pltpu.VMEM((sections, half, width), jnp.float32),
            pltpu.VMEM((sections - 1, half, width), jnp.bfloat16),
            pltpu.VMEM((sections - 1, half, width), jnp.bfloat16),
            pltpu.VMEM((half, width), jnp.float32),
            pltpu.VMEM((zones - 1, piece, width), jnp.float32),
        ]
        + dma(sections) + dma(sections - 1) + dma(zones - 1) + dma(zones - 1) + dma(zones),
        compiler_params=pltpu.CompilerParams(
            collective_id=3, has_side_effects=True, vmem_limit_bytes=40 * 2**20
        ),
    )(value)
    return out.reshape(rows, width)


def body(bases, targets, stem_weight, conv_weight, proj_weight, head_weight):
    sections = lax.axis_size("section")
    seqs = lax.axis_size("seq")
    section_number = lax.axis_index("section")
    batches, row_count, bin_width = bases.shape
    channels = stem_weight.shape[1]
    length = row_count * seqs
    factor = 1.0 / math.sqrt(batches * lax.axis_size("dp") * length)
    unit = length // 2**sections
    local_q = row_count // unit
    blocks = length // unit
    columns = batches * unit // (seqs * sections)

    paired = seqs == 2 and batches == seqs and columns % 16 == 0

    if paired:
        conv_all, proj_all = gather_weights(
            conv_weight.reshape(2, -1, conv_weight.shape[-1]),
            proj_weight.reshape(2, -1, channels),
            sections,
        )
        conv_all = conv_all.reshape((sections,) + conv_weight.shape[1:])
        proj_all = proj_all.reshape((sections,) + proj_weight.shape[1:])
    else:
        conv_all = lax.all_gather(conv_weight, "section", axis=0, tiled=True)
        proj_all = lax.all_gather(proj_weight, "section", axis=0, tiled=True)

    def to_chains(value):
        value = lax.all_to_all(value, "seq", split_axis=1, concat_axis=0, tiled=True)
        return value.reshape(blocks * columns, value.shape[-1])

    own = bases.reshape(batches, local_q, unit, bin_width).transpose(1, 0, 2, 3)
    own = own.reshape(local_q, seqs, sections, columns, bin_width)
    own = lax.dynamic_index_in_dim(own, section_number, 2, keepdims=False)
    picked = to_chains(own.astype(jnp.bfloat16))
    onehot = jnp.concatenate([(picked == c).astype(jnp.bfloat16) for c in range(4)], 1)
    stem = stem_weight.reshape(bin_width, 4, channels).transpose(1, 0, 2).reshape(-1, channels)
    state = jnp.dot(onehot, stem, preferred_element_type=jnp.float32).astype(jnp.bfloat16)

    saved = []
    for layer in range(sections):
        by = columns * 2**layer
        taps = conv_all[layer].reshape(-1, conv_all.shape[-1])
        hidden = gelu_value(state.astype(jnp.float32)).astype(jnp.bfloat16)
        wide = jnp.concatenate([shift_rows(hidden, by), hidden, shift_rows(hidden, -by)], 1)
        inner_sum = jnp.dot(wide, taps, preferred_element_type=jnp.float32)
        active = gelu_value(inner_sum).astype(jnp.bfloat16)
        update = jnp.dot(active, proj_all[layer], preferred_element_type=jnp.float32)
        saved.append((state, wide, inner_sum, active))
        state = (state.astype(jnp.float32) + update).astype(jnp.bfloat16)

    lifted = gelu_value(state.astype(jnp.float32)).astype(jnp.bfloat16)
    if paired:
        lifted = lifted.reshape(seqs, local_q, columns, channels)
        lifted = exchange(lifted, sections, seqs, columns, True)
    else:
        lifted = lifted.reshape(seqs, local_q, 1, columns, channels)
        lifted = lax.all_to_all(lifted, "seq", split_axis=0, concat_axis=2, tiled=True)
        lifted = lifted.reshape(local_q, seqs, 1, columns, channels)
        lifted = lax.all_gather(lifted, "section", axis=2, tiled=True)
        lifted = lifted.reshape(local_q, batches, unit, channels).transpose(1, 0, 2, 3)
    lifted = lifted.reshape(batches * row_count, channels)

    logits = jnp.dot(lifted, head_weight, preferred_element_type=jnp.float32)
    counts = targets.reshape(batches * row_count, targets.shape[2]).astype(jnp.float32)
    slope = ((jnp.exp(logits) - counts) * factor).astype(jnp.bfloat16)
    head_sum = lax.psum(contract_rows(lifted, slope), ("seq", "dp"))
    lift_part = times_transposed(slope, head_weight)

    if paired:
        lift_part = lift_part.astype(jnp.bfloat16).reshape(batches, local_q, unit, channels)
        terms = exchange(lift_part, sections, seqs, columns, False)
        lift_grad = terms.astype(jnp.float32).sum(0).reshape(blocks * columns, channels)
    else:
        lift_part = lift_part.reshape(batches, local_q, unit, channels).transpose(1, 0, 2, 3)
        lift_part = lift_part.reshape(local_q, seqs, sections, columns, channels)
        lift_part = lax.psum_scatter(lift_part, "section", scatter_dimension=2, tiled=True)
        lift_grad = to_chains(lift_part.reshape(local_q, seqs, columns, channels))

    grad = (lift_grad * gelu_slope(state.astype(jnp.float32))).astype(jnp.bfloat16)
    parts = []
    for layer in reversed(range(sections)):
        by = columns * 2**layer
        start_state, wide, inner_sum, active = saved[layer]
        kernel = conv_all[layer]
        proj_part = contract_rows(active, grad)
        active_grad = times_transposed(grad, proj_all[layer])
        inner_grad = (active_grad * gelu_slope(inner_sum)).astype(jnp.bfloat16)
        parts.append(jnp.concatenate([contract_rows(inner_grad, wide), proj_part], 1))
        wide_grad = jnp.concatenate(
            [shift_rows(inner_grad, -by), inner_grad, shift_rows(inner_grad, by)], 1
        )
        turned = kernel.transpose(0, 2, 1).reshape(-1, channels)
        hidden_grad = jnp.dot(wide_grad, turned, preferred_element_type=jnp.float32)
        grad = (
            grad.astype(jnp.float32) + hidden_grad * gelu_slope(start_state.astype(jnp.float32))
        ).astype(jnp.bfloat16)
    parts = jnp.stack(parts[::-1])
    zones = lax.axis_size("dp")
    if paired and zones > 1 and parts.shape[1] % (16 * zones) == 0:
        total = sum_gradients(parts, sections, zones)
    else:
        total = lax.psum_scatter(parts, "section", scatter_dimension=0, tiled=True)
        total = lax.psum(total[0], ("seq", "dp"))
    taps_width = total.shape[1] - channels
    conv_sum = total[:, :taps_width].T.reshape(conv_weight.shape)
    return conv_sum, total[:, taps_width:][None], head_sum


def solution(mesh):
    in_specs = (
        P("dp", "seq", None),
        P("dp", "seq", "section"),
        P(),
        P("section", None, None, None),
        P("section", None, None),
        P(None, "section"),
    )
    out_specs = (P("section", None, None, None), P("section", None, None), P(None, "section"))
    return jax.shard_map(body, mesh=mesh, in_specs=in_specs, out_specs=out_specs, check_vma=False)
```

```python
import math

import jax
import jax.numpy as jnp
from jax import lax
from jax.experimental import pallas as pl
from jax.experimental.pallas import tpu as pltpu
from jax.sharding import PartitionSpec as P

SQRT_TWO_OVER_PI = 0.7978845608028654
CUBIC_TERM = 0.044715


def gelu_value(inputs):
    return (
        0.5
        * inputs
        * (1.0 + jnp.tanh(SQRT_TWO_OVER_PI * (inputs + CUBIC_TERM * inputs * inputs * inputs)))
    )


def gelu_slope(inputs):
    tangent = jnp.tanh(SQRT_TWO_OVER_PI * (inputs + CUBIC_TERM * inputs * inputs * inputs))
    return 0.5 * (1.0 + tangent) + 0.5 * inputs * (1.0 - tangent * tangent) * SQRT_TWO_OVER_PI * (
        1.0 + 3.0 * CUBIC_TERM * inputs * inputs
    )


def contract_rows(left_side, right_side):
    return lax.dot_general(
        left_side, right_side, (((0,), (0,)), ((), ())), preferred_element_type=jnp.float32
    )


def times_transposed(left_side, right_side):
    return lax.dot_general(
        left_side, right_side, (((1,), (1,)), ((), ())), preferred_element_type=jnp.float32
    )


def shift_rows(value, by):
    if abs(by) >= value.shape[0]:
        return jnp.zeros_like(value)
    pad = jnp.zeros((abs(by),) + value.shape[1:], value.dtype)
    if by > 0:
        return jnp.concatenate([pad, value[:-by]], 0)
    return jnp.concatenate([value[-by:], pad], 0)


MESH = pl.DeviceIdType.MESH
ANY = pl.BlockSpec(memory_space=pl.ANY)


def greet(peers):
    barrier = pltpu.get_barrier_semaphore()
    for peer in peers:
        pl.semaphore_signal(barrier, inc=1, device_id=peer, device_id_type=MESH)
    pl.semaphore_wait(barrier, len(peers))


def remote(src, dst, send, recv, peer):
    return pltpu.make_async_remote_copy(
        src_ref=src, dst_ref=dst, send_sem=send, recv_sem=recv, device_id=peer, device_id_type=MESH
    )


def gather_inputs(bins, conv, proj, sections):
    def kernel(
        bins_ref, conv_ref, proj_ref, bins_out, conv_out, proj_out,
        send, recv, local, send2, recv2, send3, recv3,
    ):
        s, c = lax.axis_index("section"), lax.axis_index("seq")
        others = [lax.rem(s + k, sections) for k in range(1, sections)]
        partner = {"section": s, "seq": 1 - c}
        peers = [{"section": o, "seq": c} for o in others]
        greet(peers + [partner])
        pairs = ((conv_ref, conv_out), (proj_ref, proj_out))
        first, second, own = [], [], []
        for k, peer in enumerate(peers):
            for n, (src, out) in enumerate(pairs):
                first.append(remote(src.at[c], out.at[s, c], send.at[k, n], recv.at[k, n], peer))
                first[-1].start()
        for n, (src, out) in enumerate(pairs):
            own.append(pltpu.make_async_copy(src, out.at[s], local.at[n]))
            own[-1].start()
        swap = remote(bins_ref.at[1 - c], bins_out.at[c], send3, recv3, partner)
        swap.start()
        own.append(pltpu.make_async_copy(bins_ref.at[c], bins_out.at[c], local.at[2]))
        own[-1].start()
        for k in range(sections - 1):
            source = lax.rem(s + sections - 1 - k, sections)
            for n, (_, out) in enumerate(pairs):
                first[2 * k + n].wait_recv()
                piece = out.at[source, c]
                second.append(remote(piece, piece, send2.at[k, n], recv2.at[k, n], partner))
                second[-1].start()
        swap.wait()
        for copy in second:
            copy.wait()
        for copy in first:
            copy.wait_send()
        for copy in own:
            copy.wait()

    sems = pltpu.SemaphoreType.DMA((sections - 1, 2))
    return pl.pallas_call(
        kernel,
        out_shape=[
            jax.ShapeDtypeStruct(bins.shape, bins.dtype),
            jax.ShapeDtypeStruct((sections,) + conv.shape, conv.dtype),
            jax.ShapeDtypeStruct((sections,) + proj.shape, proj.dtype),
        ],
        in_specs=[ANY] * 3,
        out_specs=[ANY] * 3,
        scratch_shapes=[sems, sems, pltpu.SemaphoreType.DMA((3,)), sems, sems]
        + [pltpu.SemaphoreType.DMA] * 2,
        compiler_params=pltpu.CompilerParams(collective_id=0, has_side_effects=True),
    )(bins, conv, proj)


def exchange(value, sections, seqs, columns, to_head):
    group = sections * seqs

    def kernel(src, out, send, recv, local):
        s, c = lax.axis_index("section"), lax.axis_index("seq")
        me = s * seqs + c

        def part(ref, batch, section):
            start = pl.multiple_of(section * columns, 16)
            return ref.at[batch, :, pl.ds(start, columns), :]

        def ends(ps, pc):
            if to_head:
                return src.at[pc], part(out, c, s)
            return part(src, pc, ps), out.at[s, c]

        places = []
        for k in range(1, group):
            p = lax.rem(me + k, group)
            places.append((p // seqs, lax.rem(p, seqs)))
        peers = [{"section": ps, "seq": pc} for ps, pc in places]
        greet(peers)
        copies = []
        for k, (ps, pc) in enumerate(places):
            source, target = ends(ps, pc)
            copies.append(remote(source, target, send.at[k], recv.at[k], peers[k]))
            copies[-1].start()
        source, target = ends(s, c)
        own = pltpu.make_async_copy(source, target, local)
        own.start()
        own.wait()
        for copy in copies:
            copy.wait()

    q, channels = value.shape[1], value.shape[3]
    if to_head:
        shape = (seqs, q, sections * columns, channels)
    else:
        shape = (sections, seqs, q, columns, channels)
    sems = pltpu.SemaphoreType.DMA((group - 1,))
    return pl.pallas_call(
        kernel,
        out_shape=jax.ShapeDtypeStruct(shape, value.dtype),
        in_specs=[ANY],
        out_specs=ANY,
        scratch_shapes=[sems, sems, pltpu.SemaphoreType.DMA],
        compiler_params=pltpu.CompilerParams(
            collective_id=1 if to_head else 2, has_side_effects=True
        ),
    )(value)


def sum_gradients(value, sections, zones):
    rows, width = value.shape[1:]
    half = rows // 2
    piece = half // zones

    def kernel(
        src, out, met, wire, came, total, zcame, s0, r0, s1, r1, s2, r2, s3, r3, s4, r4
    ):
        s, c, d = (lax.axis_index(name) for name in ("section", "seq", "dp"))
        partner = {"section": s, "seq": 1 - c, "dp": d}
        order = [lax.rem(s + k, sections) for k in range(1, sections + 1)]
        across = [{"section": o, "seq": c, "dp": d} for o in order[:-1]]
        levels = [lax.rem(d + k, zones) for k in range(1, zones)]
        along = [{"section": s, "seq": c, "dp": z} for z in levels]
        greet([partner] + across + along)

        def strip(z):
            return pl.ds(pl.multiple_of(z * piece, 8), piece)

        def far(o):
            return src.at[o, pl.ds(pl.multiple_of((1 - c) * half, 8), half), :]

        def near(o):
            return src[o, pl.ds(pl.multiple_of(c * half, 8), half), :]

        pair = [remote(far(o), met.at[k], s0.at[k], r0.at[k], partner) for k, o in enumerate(order)]
        for copy in pair:
            copy.start()
        hops = []
        for k, peer in enumerate(across):
            pair[k].wait_recv()
            wire[k] = (met[k] + near(order[k])).astype(wire.dtype)
            hops.append(remote(wire.at[k], came.at[k], s1.at[k], r1.at[k], peer))
            hops[-1].start()
        pair[sections - 1].wait_recv()
        total[...] = met[sections - 1] + near(order[sections - 1])
        for k, copy in enumerate(hops):
            copy.wait_recv()
            total[...] += came[k].astype(jnp.float32)
        climbs = []
        for k, peer in enumerate(along):
            climbs.append(
                remote(total.at[strip(levels[k])], zcame.at[k], s2.at[k], r2.at[k], peer)
            )
            climbs[-1].start()
        done = total[strip(d), :]
        for k, copy in enumerate(climbs):
            copy.wait_recv()
            done = done + zcame[k]
        out[c, strip(d), :] = done

        mine = out.at[c, strip(d)]
        backs = [remote(mine, mine, s3.at[k], r3.at[k], peer) for k, peer in enumerate(along)]
        for copy in backs:
            copy.start()
        ends = [remote(mine, mine, s4.at[0], r4.at[0], partner)]
        ends[0].start()
        for k in range(zones - 1):
            backs[k].wait_recv()
            landed = out.at[c, strip(lax.rem(d + zones - 1 - k, zones))]
            ends.append(remote(landed, landed, s4.at[k + 1], r4.at[k + 1], partner))
            ends[-1].start()
        for copy in ends:
            copy.wait()
        for copy in pair + hops + climbs + backs:
            copy.wait_send()

    def dma(count):
        return [pltpu.SemaphoreType.DMA((count,))] * 2

    out = pl.pallas_call(
        kernel,
        out_shape=jax.ShapeDtypeStruct((2, half, width), jnp.float32),
        in_specs=[pl.BlockSpec(memory_space=pltpu.VMEM)],
        out_specs=pl.BlockSpec(memory_space=pltpu.VMEM),
        scratch_shapes=[
            pltpu.VMEM((sections, half, width), jnp.float32),
            pltpu.VMEM((sections - 1, half, width), jnp.bfloat16),
            pltpu.VMEM((sections - 1, half, width), jnp.bfloat16),
            pltpu.VMEM((half, width), jnp.float32),
            pltpu.VMEM((zones - 1, piece, width), jnp.float32),
        ]
        + dma(sections) + dma(sections - 1) + dma(zones - 1) + dma(zones - 1) + dma(zones),
        compiler_params=pltpu.CompilerParams(
            collective_id=3, has_side_effects=True, vmem_limit_bytes=40 * 2**20
        ),
    )(value)
    return out.reshape(rows, width)


def body(bases, targets, stem_weight, conv_weight, proj_weight, head_weight):
    sections = lax.axis_size("section")
    seqs = lax.axis_size("seq")
    section_number = lax.axis_index("section")
    batches, row_count, bin_width = bases.shape
    channels = stem_weight.shape[1]
    length = row_count * seqs
    factor = 1.0 / math.sqrt(batches * lax.axis_size("dp") * length)
    unit = length // 2**sections
    local_q = row_count // unit
    blocks = length // unit
    columns = batches * unit // (seqs * sections)

    paired = seqs == 2 and batches == seqs and columns % 16 == 0

    def to_chains(value):
        value = lax.all_to_all(value, "seq", split_axis=1, concat_axis=0, tiled=True)
        return value.reshape(blocks * columns, value.shape[-1])

    own = bases.reshape(batches, local_q, unit, bin_width).transpose(1, 0, 2, 3)
    own = own.reshape(local_q, seqs, sections, columns, bin_width)
    own = lax.dynamic_index_in_dim(own, section_number, 2, keepdims=False)
    own = own.astype(jnp.bfloat16)
    if paired:
        picked, conv_all, proj_all = gather_inputs(
            own.transpose(1, 0, 2, 3),
            conv_weight.reshape(2, -1, conv_weight.shape[-1]),
            proj_weight.reshape(2, -1, channels),
            sections,
        )
        conv_all = conv_all.reshape((sections,) + conv_weight.shape[1:])
        proj_all = proj_all.reshape((sections,) + proj_weight.shape[1:])
        picked = picked.reshape(blocks * columns, bin_width)
    else:
        conv_all = lax.all_gather(conv_weight, "section", axis=0, tiled=True)
        proj_all = lax.all_gather(proj_weight, "section", axis=0, tiled=True)
        picked = to_chains(own)
    onehot = jnp.concatenate([(picked == c).astype(jnp.bfloat16) for c in range(4)], 1)
    stem = stem_weight.reshape(bin_width, 4, channels).transpose(1, 0, 2).reshape(-1, channels)
    state = jnp.dot(onehot, stem, preferred_element_type=jnp.float32).astype(jnp.bfloat16)

    saved = []
    for layer in range(sections):
        by = columns * 2**layer
        taps = conv_all[layer].reshape(-1, conv_all.shape[-1])
        hidden = gelu_value(state.astype(jnp.float32)).astype(jnp.bfloat16)
        wide = jnp.concatenate([shift_rows(hidden, by), hidden, shift_rows(hidden, -by)], 1)
        inner_sum = jnp.dot(wide, taps, preferred_element_type=jnp.float32)
        active = gelu_value(inner_sum).astype(jnp.bfloat16)
        update = jnp.dot(active, proj_all[layer], preferred_element_type=jnp.float32)
        saved.append((state, wide, inner_sum, active))
        state = (state.astype(jnp.float32) + update).astype(jnp.bfloat16)

    lifted = gelu_value(state.astype(jnp.float32)).astype(jnp.bfloat16)
    if paired:
        lifted = lifted.reshape(seqs, local_q, columns, channels)
        lifted = exchange(lifted, sections, seqs, columns, True)
    else:
        lifted = lifted.reshape(seqs, local_q, 1, columns, channels)
        lifted = lax.all_to_all(lifted, "seq", split_axis=0, concat_axis=2, tiled=True)
        lifted = lifted.reshape(local_q, seqs, 1, columns, channels)
        lifted = lax.all_gather(lifted, "section", axis=2, tiled=True)
        lifted = lifted.reshape(local_q, batches, unit, channels).transpose(1, 0, 2, 3)
    lifted = lifted.reshape(batches * row_count, channels)

    logits = jnp.dot(lifted, head_weight, preferred_element_type=jnp.float32)
    counts = targets.reshape(batches * row_count, targets.shape[2]).astype(jnp.float32)
    slope = ((jnp.exp(logits) - counts) * factor).astype(jnp.bfloat16)
    head_sum = lax.psum(contract_rows(lifted, slope), ("seq", "dp"))
    lift_part = times_transposed(slope, head_weight)

    if paired:
        lift_part = lift_part.astype(jnp.bfloat16).reshape(batches, local_q, unit, channels)
        terms = exchange(lift_part, sections, seqs, columns, False)
        lift_grad = terms.astype(jnp.float32).sum(0).reshape(blocks * columns, channels)
    else:
        lift_part = lift_part.reshape(batches, local_q, unit, channels).transpose(1, 0, 2, 3)
        lift_part = lift_part.reshape(local_q, seqs, sections, columns, channels)
        lift_part = lax.psum_scatter(lift_part, "section", scatter_dimension=2, tiled=True)
        lift_grad = to_chains(lift_part.reshape(local_q, seqs, columns, channels))

    grad = (lift_grad * gelu_slope(state.astype(jnp.float32))).astype(jnp.bfloat16)
    parts = []
    for layer in reversed(range(sections)):
        by = columns * 2**layer
        start_state, wide, inner_sum, active = saved[layer]
        kernel = conv_all[layer]
        proj_part = contract_rows(active, grad)
        active_grad = times_transposed(grad, proj_all[layer])
        inner_grad = (active_grad * gelu_slope(inner_sum)).astype(jnp.bfloat16)
        parts.append(jnp.concatenate([contract_rows(inner_grad, wide), proj_part], 1))
        wide_grad = jnp.concatenate(
            [shift_rows(inner_grad, -by), inner_grad, shift_rows(inner_grad, by)], 1
        )
        turned = kernel.transpose(0, 2, 1).reshape(-1, channels)
        hidden_grad = jnp.dot(wide_grad, turned, preferred_element_type=jnp.float32)
        grad = (
            grad.astype(jnp.float32) + hidden_grad * gelu_slope(start_state.astype(jnp.float32))
        ).astype(jnp.bfloat16)
    parts = jnp.stack(parts[::-1])
    zones = lax.axis_size("dp")
    if paired and zones > 1 and parts.shape[1] % (16 * zones) == 0:
        total = sum_gradients(parts, sections, zones)
    else:
        total = lax.psum_scatter(parts, "section", scatter_dimension=0, tiled=True)
        total = lax.psum(total[0], ("seq", "dp"))
    taps_width = total.shape[1] - channels
    conv_sum = total[:, :taps_width].T.reshape(conv_weight.shape)
    return conv_sum, total[:, taps_width:][None], head_sum


def solution(mesh):
    in_specs = (
        P("dp", "seq", None),
        P("dp", "seq", "section"),
        P(),
        P("section", None, None, None),
        P("section", None, None),
        P(None, "section"),
    )
    out_specs = (P("section", None, None, None), P("section", None, None), P(None, "section"))
    return jax.shard_map(body, mesh=mesh, in_specs=in_specs, out_specs=out_specs, check_vma=False)
```

```python
import math

import jax
import jax.numpy as jnp
from jax import lax
from jax.experimental import pallas as pl
from jax.experimental.pallas import tpu as pltpu
from jax.sharding import PartitionSpec as P

SQRT_TWO_OVER_PI = 0.7978845608028654
CUBIC_TERM = 0.044715


def gelu_value(inputs):
    return (
        0.5
        * inputs
        * (1.0 + jnp.tanh(SQRT_TWO_OVER_PI * (inputs + CUBIC_TERM * inputs * inputs * inputs)))
    )


def gelu_slope(inputs):
    tangent = jnp.tanh(SQRT_TWO_OVER_PI * (inputs + CUBIC_TERM * inputs * inputs * inputs))
    return 0.5 * (1.0 + tangent) + 0.5 * inputs * (1.0 - tangent * tangent) * SQRT_TWO_OVER_PI * (
        1.0 + 3.0 * CUBIC_TERM * inputs * inputs
    )


def contract_rows(left_side, right_side):
    return lax.dot_general(
        left_side, right_side, (((0,), (0,)), ((), ())), preferred_element_type=jnp.float32
    )


def times_transposed(left_side, right_side):
    return lax.dot_general(
        left_side, right_side, (((1,), (1,)), ((), ())), preferred_element_type=jnp.float32
    )


def shift_rows(value, by):
    if abs(by) >= value.shape[0]:
        return jnp.zeros_like(value)
    pad = jnp.zeros((abs(by),) + value.shape[1:], value.dtype)
    if by > 0:
        return jnp.concatenate([pad, value[:-by]], 0)
    return jnp.concatenate([value[-by:], pad], 0)


MESH = pl.DeviceIdType.MESH
ANY = pl.BlockSpec(memory_space=pl.ANY)


def greet(peers):
    barrier = pltpu.get_barrier_semaphore()
    for peer in peers:
        pl.semaphore_signal(barrier, inc=1, device_id=peer, device_id_type=MESH)
    pl.semaphore_wait(barrier, len(peers))


def remote(src, dst, send, recv, peer):
    return pltpu.make_async_remote_copy(
        src_ref=src, dst_ref=dst, send_sem=send, recv_sem=recv, device_id=peer, device_id_type=MESH
    )


def gather_weights(conv, proj, sections):
    def kernel(conv_ref, proj_ref, conv_out, proj_out, send, recv, local, send2, recv2):
        s, c = lax.axis_index("section"), lax.axis_index("seq")
        others = [lax.rem(s + k, sections) for k in range(1, sections)]
        partner = {"section": s, "seq": 1 - c}
        peers = [{"section": o, "seq": c} for o in others]
        greet(peers + [partner])
        pairs = ((conv_ref, conv_out), (proj_ref, proj_out))
        first, second, own = [], [], []
        for k, peer in enumerate(peers):
            for n, (src, out) in enumerate(pairs):
                first.append(remote(src.at[c], out.at[s, c], send.at[k, n], recv.at[k, n], peer))
                first[-1].start()
        for n, (src, out) in enumerate(pairs):
            own.append(pltpu.make_async_copy(src, out.at[s], local.at[n]))
            own[-1].start()
        for k in range(sections - 1):
            source = lax.rem(s + sections - 1 - k, sections)
            for n, (_, out) in enumerate(pairs):
                first[2 * k + n].wait_recv()
                piece = out.at[source, c]
                second.append(remote(piece, piece, send2.at[k, n], recv2.at[k, n], partner))
                second[-1].start()
        for copy in second:
            copy.wait()
        for copy in first:
            copy.wait_send()
        for copy in own:
            copy.wait()

    sems = pltpu.SemaphoreType.DMA((sections - 1, 2))
    return pl.pallas_call(
        kernel,
        out_shape=[
            jax.ShapeDtypeStruct((sections,) + conv.shape, conv.dtype),
            jax.ShapeDtypeStruct((sections,) + proj.shape, proj.dtype),
        ],
        in_specs=[ANY] * 2,
        out_specs=[ANY] * 2,
        scratch_shapes=[sems, sems, pltpu.SemaphoreType.DMA((2,)), sems, sems],
        compiler_params=pltpu.CompilerParams(collective_id=0, has_side_effects=True),
    )(conv, proj)


def exchange(value, sections, seqs, columns, to_head):
    group = sections * seqs

    def kernel(src, out, send, recv, local):
        s, c = lax.axis_index("section"), lax.axis_index("seq")
        me = s * seqs + c

        def part(ref, batch, section):
            start = pl.multiple_of(section * columns, 16)
            return ref.at[batch, :, pl.ds(start, columns), :]

        def ends(ps, pc):
            if to_head:
                return src.at[pc], part(out, c, s)
            return part(src, pc, ps), out.at[s, c]

        places = []
        for k in range(1, group):
            p = lax.rem(me + k, group)
            places.append((p // seqs, lax.rem(p, seqs)))
        peers = [{"section": ps, "seq": pc} for ps, pc in places]
        greet(peers)
        copies = []
        for k, (ps, pc) in enumerate(places):
            source, target = ends(ps, pc)
            copies.append(remote(source, target, send.at[k], recv.at[k], peers[k]))
            copies[-1].start()
        source, target = ends(s, c)
        own = pltpu.make_async_copy(source, target, local)
        own.start()
        own.wait()
        for copy in copies:
            copy.wait()

    q, channels = value.shape[1], value.shape[3]
    if to_head:
        shape = (seqs, q, sections * columns, channels)
    else:
        shape = (sections, seqs, q, columns, channels)
    sems = pltpu.SemaphoreType.DMA((group - 1,))
    return pl.pallas_call(
        kernel,
        out_shape=jax.ShapeDtypeStruct(shape, value.dtype),
        in_specs=[pl.BlockSpec(memory_space=pltpu.VMEM)],
        out_specs=pl.BlockSpec(memory_space=pltpu.VMEM),
        scratch_shapes=[sems, sems, pltpu.SemaphoreType.DMA],
        compiler_params=pltpu.CompilerParams(
            collective_id=1 if to_head else 2, has_side_effects=True, vmem_limit_bytes=16 * 2**20
        ),
    )(value)


def sum_gradients(value, sections, zones):
    rows, width = value.shape[1:]
    half = rows // 2
    piece = half // zones

    def kernel(
        src, out, met, wire, came, total, zcame, s0, r0, s1, r1, s2, r2, s3, r3, s4, r4
    ):
        s, c, d = (lax.axis_index(name) for name in ("section", "seq", "dp"))
        partner = {"section": s, "seq": 1 - c, "dp": d}
        order = [lax.rem(s + k, sections) for k in range(1, sections + 1)]
        across = [{"section": o, "seq": c, "dp": d} for o in order[:-1]]
        levels = [lax.rem(d + k, zones) for k in range(1, zones)]
        along = [{"section": s, "seq": c, "dp": z} for z in levels]
        greet([partner] + across + along)

        def strip(z):
            return pl.ds(pl.multiple_of(z * piece, 8), piece)

        def far(o):
            return src.at[o, pl.ds(pl.multiple_of((1 - c) * half, 8), half), :]

        def near(o):
            return src[o, pl.ds(pl.multiple_of(c * half, 8), half), :]

        pair = [remote(far(o), met.at[k], s0.at[k], r0.at[k], partner) for k, o in enumerate(order)]
        for copy in pair:
            copy.start()
        hops = []
        for k, peer in enumerate(across):
            pair[k].wait_recv()
            wire[k] = (met[k] + near(order[k])).astype(wire.dtype)
            hops.append(remote(wire.at[k], came.at[k], s1.at[k], r1.at[k], peer))
            hops[-1].start()
        pair[sections - 1].wait_recv()
        total[...] = met[sections - 1] + near(order[sections - 1])
        for k, copy in enumerate(hops):
            copy.wait_recv()
            total[...] += came[k].astype(jnp.float32)
        climbs = []
        for k, peer in enumerate(along):
            climbs.append(
                remote(total.at[strip(levels[k])], zcame.at[k], s2.at[k], r2.at[k], peer)
            )
            climbs[-1].start()
        done = total[strip(d), :]
        for k, copy in enumerate(climbs):
            copy.wait_recv()
            done = done + zcame[k]
        out[c, strip(d), :] = done

        mine = out.at[c, strip(d)]
        backs = [remote(mine, mine, s3.at[k], r3.at[k], peer) for k, peer in enumerate(along)]
        for copy in backs:
            copy.start()
        ends = [remote(mine, mine, s4.at[0], r4.at[0], partner)]
        ends[0].start()
        for k in range(zones - 1):
            backs[k].wait_recv()
            landed = out.at[c, strip(lax.rem(d + zones - 1 - k, zones))]
            ends.append(remote(landed, landed, s4.at[k + 1], r4.at[k + 1], partner))
            ends[-1].start()
        for copy in ends:
            copy.wait()
        for copy in pair + hops + climbs + backs:
            copy.wait_send()

    def dma(count):
        return [pltpu.SemaphoreType.DMA((count,))] * 2

    out = pl.pallas_call(
        kernel,
        out_shape=jax.ShapeDtypeStruct((2, half, width), jnp.float32),
        in_specs=[pl.BlockSpec(memory_space=pltpu.VMEM)],
        out_specs=pl.BlockSpec(memory_space=pltpu.VMEM),
        scratch_shapes=[
            pltpu.VMEM((sections, half, width), jnp.float32),
            pltpu.VMEM((sections - 1, half, width), jnp.bfloat16),
            pltpu.VMEM((sections - 1, half, width), jnp.bfloat16),
            pltpu.VMEM((half, width), jnp.float32),
            pltpu.VMEM((zones - 1, piece, width), jnp.float32),
        ]
        + dma(sections) + dma(sections - 1) + dma(zones - 1) + dma(zones - 1) + dma(zones),
        compiler_params=pltpu.CompilerParams(
            collective_id=3, has_side_effects=True, vmem_limit_bytes=40 * 2**20
        ),
    )(value)
    return out.reshape(rows, width)


def body(bases, targets, stem_weight, conv_weight, proj_weight, head_weight):
    sections = lax.axis_size("section")
    seqs = lax.axis_size("seq")
    section_number = lax.axis_index("section")
    batches, row_count, bin_width = bases.shape
    channels = stem_weight.shape[1]
    length = row_count * seqs
    factor = 1.0 / math.sqrt(batches * lax.axis_size("dp") * length)
    unit = length // 2**sections
    local_q = row_count // unit
    blocks = length // unit
    columns = batches * unit // (seqs * sections)

    paired = seqs == 2 and batches == seqs and columns % 16 == 0

    if paired:
        conv_all, proj_all = gather_weights(
            conv_weight.reshape(2, -1, conv_weight.shape[-1]),
            proj_weight.reshape(2, -1, channels),
            sections,
        )
        conv_all = conv_all.reshape((sections,) + conv_weight.shape[1:])
        proj_all = proj_all.reshape((sections,) + proj_weight.shape[1:])
    else:
        conv_all = lax.all_gather(conv_weight, "section", axis=0, tiled=True)
        proj_all = lax.all_gather(proj_weight, "section", axis=0, tiled=True)

    def to_chains(value):
        value = lax.all_to_all(value, "seq", split_axis=1, concat_axis=0, tiled=True)
        return value.reshape(blocks * columns, value.shape[-1])

    own = bases.reshape(batches, local_q, unit, bin_width).transpose(1, 0, 2, 3)
    own = own.reshape(local_q, seqs, sections, columns, bin_width)
    own = lax.dynamic_index_in_dim(own, section_number, 2, keepdims=False)
    picked = to_chains(own.astype(jnp.bfloat16))
    onehot = jnp.concatenate([(picked == c).astype(jnp.bfloat16) for c in range(4)], 1)
    stem = stem_weight.reshape(bin_width, 4, channels).transpose(1, 0, 2).reshape(-1, channels)
    state = jnp.dot(onehot, stem, preferred_element_type=jnp.float32).astype(jnp.bfloat16)

    saved = []
    for layer in range(sections):
        by = columns * 2**layer
        taps = conv_all[layer].reshape(-1, conv_all.shape[-1])
        hidden = gelu_value(state.astype(jnp.float32)).astype(jnp.bfloat16)
        wide = jnp.concatenate([shift_rows(hidden, by), hidden, shift_rows(hidden, -by)], 1)
        inner_sum = jnp.dot(wide, taps, preferred_element_type=jnp.float32)
        active = gelu_value(inner_sum).astype(jnp.bfloat16)
        update = jnp.dot(active, proj_all[layer], preferred_element_type=jnp.float32)
        saved.append((state, wide, inner_sum, active))
        state = (state.astype(jnp.float32) + update).astype(jnp.bfloat16)

    lifted = gelu_value(state.astype(jnp.float32)).astype(jnp.bfloat16)
    if paired:
        lifted = lifted.reshape(seqs, local_q, columns, channels)
        lifted = exchange(lifted, sections, seqs, columns, True)
    else:
        lifted = lifted.reshape(seqs, local_q, 1, columns, channels)
        lifted = lax.all_to_all(lifted, "seq", split_axis=0, concat_axis=2, tiled=True)
        lifted = lifted.reshape(local_q, seqs, 1, columns, channels)
        lifted = lax.all_gather(lifted, "section", axis=2, tiled=True)
        lifted = lifted.reshape(local_q, batches, unit, channels).transpose(1, 0, 2, 3)
    lifted = lifted.reshape(batches * row_count, channels)

    logits = jnp.dot(lifted, head_weight, preferred_element_type=jnp.float32)
    counts = targets.reshape(batches * row_count, targets.shape[2]).astype(jnp.float32)
    slope = ((jnp.exp(logits) - counts) * factor).astype(jnp.bfloat16)
    head_sum = lax.psum(contract_rows(lifted, slope), ("seq", "dp"))
    lift_part = times_transposed(slope, head_weight)

    if paired:
        lift_part = lift_part.astype(jnp.bfloat16).reshape(batches, local_q, unit, channels)
        terms = exchange(lift_part, sections, seqs, columns, False)
        lift_grad = terms.astype(jnp.float32).sum(0).reshape(blocks * columns, channels)
    else:
        lift_part = lift_part.reshape(batches, local_q, unit, channels).transpose(1, 0, 2, 3)
        lift_part = lift_part.reshape(local_q, seqs, sections, columns, channels)
        lift_part = lax.psum_scatter(lift_part, "section", scatter_dimension=2, tiled=True)
        lift_grad = to_chains(lift_part.reshape(local_q, seqs, columns, channels))

    grad = (lift_grad * gelu_slope(state.astype(jnp.float32))).astype(jnp.bfloat16)
    parts = []
    for layer in reversed(range(sections)):
        by = columns * 2**layer
        start_state, wide, inner_sum, active = saved[layer]
        kernel = conv_all[layer]
        proj_part = contract_rows(active, grad)
        active_grad = times_transposed(grad, proj_all[layer])
        inner_grad = (active_grad * gelu_slope(inner_sum)).astype(jnp.bfloat16)
        parts.append(jnp.concatenate([contract_rows(inner_grad, wide), proj_part], 1))
        wide_grad = jnp.concatenate(
            [shift_rows(inner_grad, -by), inner_grad, shift_rows(inner_grad, by)], 1
        )
        turned = kernel.transpose(0, 2, 1).reshape(-1, channels)
        hidden_grad = jnp.dot(wide_grad, turned, preferred_element_type=jnp.float32)
        grad = (
            grad.astype(jnp.float32) + hidden_grad * gelu_slope(start_state.astype(jnp.float32))
        ).astype(jnp.bfloat16)
    parts = jnp.stack(parts[::-1])
    zones = lax.axis_size("dp")
    if paired and zones > 1 and parts.shape[1] % (16 * zones) == 0:
        total = sum_gradients(parts, sections, zones)
    else:
        total = lax.psum_scatter(parts, "section", scatter_dimension=0, tiled=True)
        total = lax.psum(total[0], ("seq", "dp"))
    taps_width = total.shape[1] - channels
    conv_sum = total[:, :taps_width].T.reshape(conv_weight.shape)
    return conv_sum, total[:, taps_width:][None], head_sum


def solution(mesh):
    in_specs = (
        P("dp", "seq", None),
        P("dp", "seq", "section"),
        P(),
        P("section", None, None, None),
        P("section", None, None),
        P(None, "section"),
    )
    out_specs = (P("section", None, None, None), P("section", None, None), P(None, "section"))
    return jax.shard_map(body, mesh=mesh, in_specs=in_specs, out_specs=out_specs, check_vma=False)
```
